512 devices in a mesh: dp: 32 (over y, x), gene: 16 (over z, core).
Axes of the slice: x: 4, y: 8, z: 8, core: 2. Of those that a mesh axis runs over, the one named last changes fastest.
Arguments:
- labels: int32 [32768], P('dp'), may hold values from 0 to 511, as said below
- counts: int32 [32768, 16384], P('dp', 'gene'), may hold values from 0 to 39
- library_size: int32 [32768], P('dp'), may hold values from 2000 to 29999
- loadings: bfloat16 [16384, 256], P('gene'), may hold values from -0.046875 to 0.046875
Outputs:
- normalized: bfloat16 [512, 16384], P(('dp', 'gene'))
- scores: float32 [512, 256], P(('dp', 'gene'))
The draws below stay inside these ranges and needn't reach their ends.
Inputs may be any that keep to these rules, and one draw needn't show every extreme that they name: Within each device's block of 1024 cells the labels do not fall; every group has at least one cell.
All inputs are finite; a program needn't handle non-finite values.
Results may differ from the reference program's by a relative error of at most 0.0065.
Values may be sent and summed in bfloat16 or wider, within the bound.
No kernel may reach another device: no remote copies, remote signals or barrier semaphores. Data moves between devices by JAX's collectives and lax.ppermute only.
A program may use at most 64 MiB of HBM per device.

```python
import jax
import jax.numpy as jnp
from jax import lax

G = 512
GENES = 16384
K = 256
CELL_DEV = 1024
CELLS = 32768


def draw_labels(key, part):
    key = jax.random.fold_in(key, 11)
    key_one, key_two, key_three, key_four = jax.random.split(key, 4)
    shards = CELLS // CELL_DEV
    shape = (shards, CELL_DEV)
    skewed = jnp.minimum(jax.random.randint(key_one, shape, 0, G), jax.random.randint(key_two, shape, 0, G))
    skewed = jnp.minimum(skewed, jax.random.randint(key_three, shape, 0, G))
    relabel = jax.random.permutation(key_four, G)
    chosen = relabel[skewed]
    per_shard = G // shards
    position = jnp.arange(CELL_DEV, dtype=jnp.int32)[None, :]
    device_row = jnp.arange(shards, dtype=jnp.int32)[:, None]
    chosen = jnp.where(position < per_shard, device_row * per_shard + position, chosen)
    chosen = jnp.sort(chosen, axis=1)
    return chosen.reshape(-1).astype(jnp.int32)


def with_ends(array, key, smallest, high):
    longest = array.shape.index(max(array.shape))
    spots = []
    for shift in (0, 1):
        where = [jax.random.randint(jax.random.fold_in(key, axis), (), 0, length) for axis, length in enumerate(array.shape)]
        where[longest] = (where[longest] + shift) % array.shape[longest]
        spots.append(tuple(where))
    return array.at[spots[0]].set(smallest).at[spots[1]].set(high)


def block_scale(key, extent, pieces, least, largest):
    level, own = 1.0, jax.random.fold_in(key, 6)
    for dim, blocks in pieces:
        steps = jnp.exp(jax.random.uniform(jax.random.fold_in(own, dim), (blocks,), jnp.float32, least / len(pieces), largest / len(pieces)))
        level = level * jnp.repeat(steps, extent[dim] // blocks).reshape([-1 if axis == dim else 1 for axis in range(len(extent))])
    return level


def normal_values(own_key, shape, spread, limit, cuts=(), kind=jnp.bfloat16):
    drawn = spread * jax.random.normal(own_key, shape, jnp.float32)
    if cuts:
        drawn = drawn * block_scale(own_key, shape, cuts, -0.22, 0.18)
    return jnp.clip(drawn, -limit, limit).astype(kind)


def setup_inputs(seed: int = 0) -> dict:
    keys = jax.random.split(jax.random.key(seed), 5)
    return {
        "labels": draw_labels(jax.random.fold_in(keys[4], 71), 0),
        "counts": with_ends(jax.random.randint(keys[1], (CELLS, GENES), 0, 40), jax.random.fold_in(keys[1], 1), 0, 39).astype(jnp.int32),
        "library_size": with_ends(jax.random.randint(keys[2], (CELLS,), 2000, 30000), jax.random.fold_in(keys[2], 1), 2000, 29999).astype(jnp.int32),
        "loadings": normal_values(keys[3], (GENES, K), GENES ** -0.5, 0.046875, ((0, 16),)),
    }


def reference(labels, counts, library_size, loadings):
    block_rows = CELL_DEV
    block_count = CELLS // block_rows

    def add_block(summed, index):
        start = index * block_rows
        block_labels = lax.dynamic_slice_in_dim(labels, start, block_rows, 0)
        block_counts = lax.dynamic_slice_in_dim(counts, start, block_rows, 0).astype(jnp.float32)
        return summed + jax.ops.segment_sum(block_counts, block_labels, num_segments=G), None

    pseudo, _ = lax.scan(add_block, jnp.zeros((G, GENES), jnp.float32), jnp.arange(block_count, dtype=jnp.int32))
    library = jax.ops.segment_sum(library_size.astype(jnp.float32), labels, num_segments=G)
    normalized = jnp.log(1.0 + 10000.0 * pseudo / library[:, None]).astype(jnp.bfloat16)
    scores = jnp.dot(normalized, loadings, preferred_element_type=jnp.float32)
    return normalized, scores
```

```python
import jax
import jax.numpy as jnp
from jax import lax
from jax.sharding import PartitionSpec as P

G = 512
F32 = jnp.float32
BF16 = jnp.bfloat16


def split3(value):
    one = value.astype(BF16)
    rest = value - one.astype(F32)
    two = rest.astype(BF16)
    return one, two, (rest - two.astype(F32)).astype(BF16)


def shards(labels, counts, library_size, loadings):
    cells = labels.shape[0]
    genes = counts.shape[1]
    k = loadings.shape[1]
    members = lax.broadcasted_iota(jnp.int32, (G, cells), 0) == labels[None, :]
    partial_value = jnp.dot(members.astype(BF16), counts.astype(BF16), preferred_element_type=F32)
    library_part = jnp.sum(jnp.where(members, library_size.astype(F32)[None, :], 0.0), axis=1)
    lib = jnp.stack(split3(library_part), axis=1)
    sent = jnp.concatenate([partial_value.astype(BF16), jnp.pad(lib, ((0, 0), (0, 125)))], axis=1)
    got = lax.all_to_all(sent, "dp", 0, 0, tiled=True)
    summed = jnp.sum(got.reshape(32, 16, genes + 128).astype(F32), axis=0)
    pseudo = summed[:, :genes]
    library = jnp.sum(summed[:, genes:], axis=1)
    normalized = jnp.log(1.0 + 10000.0 * pseudo / library[:, None]).astype(BF16)
    partial_scores = jnp.dot(normalized, loadings, preferred_element_type=F32)
    sent = jnp.concatenate([normalized, *split3(partial_scores)], axis=1)
    got = lax.all_to_all(sent.reshape(16, -1, 128), "gene", 0, 0, tiled=True)
    rows = genes // 128
    group_major = got[:, :rows].reshape(1, 16 * genes)
    scores = jnp.sum(got[:, rows:].astype(F32).reshape(16, 3, k), axis=(0, 1))[None]
    return (group_major, scores)


def solution(mesh):
    placed = (P("dp"), P("dp", "gene"), P("dp"), P("gene", None))
    return jax.shard_map(
        shards,
        mesh=mesh,
        in_specs=placed,
        out_specs=(P(("dp", "gene"), None), P(("dp", "gene"), None)),
        check_vma=False,
    )
```

```python
import jax
import jax.numpy as jnp
from jax import lax
from jax.experimental import pallas as pl
from jax.experimental.pallas import tpu as pltpu
from jax.sharding import PartitionSpec as P

G = 512
F32 = jnp.float32
BF16 = jnp.bfloat16
LANES = 128
OWN = 16
FIRST = [[(2 * h + l) * 4 + x for l in range(2) for x in range(4)] for h in range(4)]
SECOND = [[(2 * h + l) * 4 + x for h in range(4)] for l in range(2) for x in range(4)]
VMEM = pl.BlockSpec(memory_space=pltpu.VMEM)
LIMIT = 48 * 1024 * 1024


def split3(value):
    one = value.astype(BF16).astype(F32)
    two = (value - one).astype(BF16).astype(F32)
    return one, two, ((value - one) - two).astype(BF16).astype(F32)


def in_lanes(pieces, lane):
    return jnp.where(lane == 0, pieces[0], jnp.where(lane == 1, pieces[1], jnp.where(lane == 2, pieces[2], 0.0)))


def sums_kernel(labels_ref, lib_ref, counts_ref, out_ref, members_ref):
    step = pl.program_id(0)
    cells = counts_ref.shape[0]
    width = counts_ref.shape[1]
    tiles = width // LANES

    @pl.when(step == 0)
    def _():
        group = lax.broadcasted_iota(jnp.int32, (G, cells), 0)
        members_ref[...] = (group == labels_ref[...].reshape(1, cells)).astype(F32).astype(BF16)
        size = lib_ref[...].reshape(1, cells)
        high = size // 256
        low = size - high * 256
        part = jnp.where(lax.broadcasted_iota(jnp.int32, (2 * LANES, cells), 0) < LANES, high, low)
        both = lax.dot_general(
            members_ref[...], part.astype(F32).astype(BF16), (((1,), (1,)), ((), ())), preferred_element_type=F32
        )
        total = both[:, :LANES] * 256.0 + both[:, LANES:]
        lane = lax.broadcasted_iota(jnp.int32, (G, LANES), 1)
        placed = in_lanes(split3(total), lane % 4)
        lane = lax.broadcasted_iota(jnp.int32, (OWN, LANES), 1) // 4
        for m in range(8):
            tile = jnp.zeros((OWN, LANES), F32)
            for h in range(4):
                at = (h * 8 + m) * OWN
                tile = jnp.where(lane == h, placed[at : at + OWN], tile)
            out_ref[m, out_ref.shape[1] - OWN :, :] = tile.astype(BF16)

    sums = jnp.dot(members_ref[...], counts_ref[...].astype(F32).astype(BF16), preferred_element_type=F32)
    sums = sums.astype(BF16)
    for m in range(8):
        for t in range(tiles):
            for h in range(4):
                at = (h * 8 + m) * OWN
                row = pl.multiple_of((step * tiles + t) * 64, 64) + h * OWN
                out_ref[m, pl.ds(row, OWN), :] = sums[at : at + OWN, t * LANES : (t + 1) * LANES]


def middle_kernel(got_ref, out_ref):
    tiles = (got_ref.shape[1] - OWN) // 64

    def added(row):
        return sum(got_ref[m, row : row + OWN, :].astype(F32) for m in range(8))

    lane = lax.broadcasted_iota(jnp.int32, (OWN, LANES), 1)
    library = added(tiles * 64)
    for h in range(4):
        for t in range(tiles):
            out_ref[h, t * OWN : (t + 1) * OWN, :] = added(t * 64 + h * OWN).astype(BF16)
        mine = jnp.sum(jnp.where(lane // 4 == h, library, 0.0), axis=1, keepdims=True)
        out_ref[h, tiles * OWN :, :] = in_lanes(split3(mine), lane).astype(BF16)


def project_kernel(got_ref, loadings_ref, out_ref, rows_ref):
    tiles = got_ref.shape[1] // OWN - 1
    halves = loadings_ref.shape[1] // LANES

    def added(t):
        return sum(got_ref[h, t * OWN : (t + 1) * OWN, :].astype(F32) for h in range(4))

    library = jnp.sum(added(tiles), axis=1, keepdims=True)
    scores = jnp.zeros((OWN, loadings_ref.shape[1]), F32)
    rows_ref[...] = jnp.zeros_like(rows_ref)
    profile = []
    for t in range(tiles):
        normalized = jnp.log(1.0 + 10000.0 * added(t) / library).astype(BF16)
        rows_ref[pl.ds(t, OWN, stride=OWN), :] = normalized.astype(F32)
        profile.append(normalized)
    scores = jnp.dot(jnp.concatenate(profile, axis=1), loadings_ref[...], preferred_element_type=F32)
    for p, piece in enumerate(split3(scores)):
        for k in range(halves):
            at = tiles + p * halves + k
            rows_ref[pl.ds(at, OWN, stride=OWN), :] = piece[:, k * LANES : (k + 1) * LANES]
    for j in range(OWN):
        out_ref[j] = rows_ref[j * OWN : (j + 1) * OWN, :].astype(BF16)


def finish_kernel(got_ref, profile_ref, scores_ref):
    halves = scores_ref.shape[1] // LANES
    tiles = profile_ref.shape[1] // (got_ref.shape[0] * LANES)
    total = jnp.zeros((OWN, LANES), F32)
    for source in range(got_ref.shape[0]):
        block = got_ref[source].astype(F32)
        total += block
        for t in range(tiles):
            at = (source * tiles + t) * LANES
            profile_ref[:, at : at + LANES] = block[t : t + 1].astype(BF16)
    for k in range(halves):
        scores_ref[:, k * LANES : (k + 1) * LANES] = sum(
            total[tiles + p * halves + k : tiles + p * halves + k + 1] for p in range(3)
        )


def shards(labels, counts, library_size, loadings):
    cells, genes = counts.shape
    k = loadings.shape[1]
    tiles = genes // LANES
    width = 256
    sent = pl.pallas_call(
        sums_kernel,
        grid=(genes // width,),
        in_specs=[
            pl.BlockSpec((cells,), lambda i: (0,)),
            pl.BlockSpec((cells,), lambda i: (0,)),
            pl.BlockSpec((cells, width), lambda i: (0, i)),
        ],
        out_specs=pl.BlockSpec((8, tiles * 64 + OWN, LANES), lambda i: (0, 0, 0)),
        out_shape=jax.ShapeDtypeStruct((8, tiles * 64 + OWN, LANES), BF16),
        scratch_shapes=[pltpu.VMEM((G, cells), BF16)],
        compiler_params=pltpu.CompilerParams(vmem_limit_bytes=LIMIT),
    )(labels, library_size, counts)
    got = lax.all_to_all(sent, "dp", 0, 0, tiled=True, axis_index_groups=FIRST)
    sent = pl.pallas_call(
        middle_kernel,
        in_specs=[VMEM],
        out_specs=VMEM,
        out_shape=jax.ShapeDtypeStruct((4, tiles * OWN + OWN, LANES), BF16),
        compiler_params=pltpu.CompilerParams(vmem_limit_bytes=LIMIT),
    )(got)
    got = lax.all_to_all(sent, "dp", 0, 0, tiled=True, axis_index_groups=SECOND)
    sent = pl.pallas_call(
        project_kernel,
        in_specs=[VMEM, VMEM],
        out_specs=VMEM,
        out_shape=jax.ShapeDtypeStruct((16, OWN, LANES), BF16),
        scratch_shapes=[pltpu.VMEM((16 * OWN, LANES), F32)],
        compiler_params=pltpu.CompilerParams(vmem_limit_bytes=LIMIT),
    )(got, loadings)
    got = lax.all_to_all(sent, "gene", 0, 0, tiled=True)
    return pl.pallas_call(
        finish_kernel,
        in_specs=[VMEM],
        out_specs=(VMEM, VMEM),
        out_shape=(
            jax.ShapeDtypeStruct((1, 16 * genes), BF16),
            jax.ShapeDtypeStruct((1, k), F32),
        ),
        compiler_params=pltpu.CompilerParams(vmem_limit_bytes=LIMIT),
    )(got)


def solution(mesh):
    placed = (P("dp"), P("dp", "gene"), P("dp"), P("gene", None))
    return jax.shard_map(
        shards,
        mesh=mesh,
        in_specs=placed,
        out_specs=(P(("dp", "gene"), None), P(("dp", "gene"), None)),
        check_vma=False,
    )
```

```python
import jax
import jax.numpy as jnp
from jax import lax
from jax.experimental import pallas as pl
from jax.experimental.pallas import tpu as pltpu
from jax.sharding import PartitionSpec as P

G = 512
F32 = jnp.float32
BF16 = jnp.bfloat16
LANES = 128
OWN = 16
SETS = ((1, 2, 4, 7), (0, 3, 5, 6))
FIRST = [[y[h] * 4 + x for y in SETS for x in range(4)] for h in range(4)]
SECOND = [[y[h] * 4 + x for h in range(4)] for y in SETS for x in range(4)]
VMEM = pl.BlockSpec(memory_space=pltpu.VMEM)
HBM = pl.BlockSpec(memory_space=pltpu.HBM)
LIMIT = 48 * 1024 * 1024


def split3(value):
    one = value.astype(BF16).astype(F32)
    two = (value - one).astype(BF16).astype(F32)
    return one, two, ((value - one) - two).astype(BF16).astype(F32)


def in_lanes(pieces, lane):
    return jnp.where(lane == 0, pieces[0], jnp.where(lane == 1, pieces[1], jnp.where(lane == 2, pieces[2], 0.0)))


def sums_kernel(
    labels_hbm,
    lib_hbm,
    counts_hbm,
    out_ref,
    labels_ref,
    lib_ref,
    counts_ref,
    members_ref,
    part_ref,
    tile_ref,
    small_sems,
    sems,
):
    blocks, cells, width = counts_ref.shape
    tiles = width // LANES
    span = tiles * 64
    chunk = G // 4
    end = blocks * span

    def arriving(b):
        columns = pl.ds(pl.multiple_of(b * width, width), width)
        return pltpu.make_async_copy(counts_hbm.at[:, columns], counts_ref.at[b], sems.at[b])

    labels_copy = pltpu.make_async_copy(labels_hbm, labels_ref, small_sems.at[0])
    lib_copy = pltpu.make_async_copy(lib_hbm, lib_ref, small_sems.at[1])
    labels_copy.start()
    lib_copy.start()

    @pl.loop(0, blocks)
    def _(b):
        arriving(b).start()

    tile_ref[...] = jnp.zeros_like(tile_ref)
    labels_copy.wait()
    lib_copy.wait()
    size = lib_ref[...].reshape(1, cells)
    high = size // 256
    part_ref[:LANES] = jnp.broadcast_to(high.astype(F32), (LANES, cells)).astype(BF16)
    part_ref[LANES:] = jnp.broadcast_to((size - high * 256).astype(F32), (LANES, cells)).astype(BF16)

    @pl.loop(0, 4)
    def _(h):
        at = pl.multiple_of(h * chunk, chunk)
        swap = jnp.where((h == 0) | (h == 3), chunk // 2, 0)
        group = (lax.broadcasted_iota(jnp.int32, (chunk, cells), 0) ^ swap) + at
        members = (group == labels_ref[...].reshape(1, cells)).astype(F32).astype(BF16)
        members_ref[pl.ds(at, chunk), :] = members
        both = lax.dot_general(members, part_ref[...], (((1,), (1,)), ((), ())), preferred_element_type=F32)
        lane = lax.broadcasted_iota(jnp.int32, (chunk, LANES), 1)
        placed = in_lanes(split3(both[:, :LANES] * 256.0 + both[:, LANES:]), lane % 4)
        tile_ref[...] = jnp.where(lane // 4 == h, placed, tile_ref[...])

    out_ref[:, end:, :] = tile_ref[...].astype(BF16).reshape(8, OWN, LANES)

    @pl.loop(0, blocks)
    def _(b):
        arriving(b).wait()
        sums = jnp.dot(members_ref[...], counts_ref[b].astype(F32).astype(BF16), preferred_element_type=F32)
        sums = sums.astype(BF16)
        for t in range(tiles):
            for h in range(4):
                row = pl.multiple_of(b * span, span) + t * 64 + h * OWN
                part = sums[h * chunk : (h + 1) * chunk, t * LANES : (t + 1) * LANES]
                out_ref[:, pl.ds(row, OWN), :] = part.reshape(8, OWN, LANES)


def middle_kernel(got_ref, out_ref):
    tiles = (got_ref.shape[1] - OWN) // 64

    def added(row):
        return sum(got_ref[m, row : row + OWN, :].astype(F32) for m in range(8))

    lane = lax.broadcasted_iota(jnp.int32, (OWN, LANES), 1)
    library = added(tiles * 64)
    for h in range(4):
        for t in range(tiles):
            out_ref[h, t * OWN : (t + 1) * OWN, :] = added(t * 64 + h * OWN).astype(BF16)
        mine = jnp.sum(jnp.where(lane // 4 == h, library, 0.0), axis=1, keepdims=True)
        out_ref[h, tiles * OWN :, :] = in_lanes(split3(mine), lane).astype(BF16)


def project_kernel(got_ref, loadings_ref, out_ref, rows_ref):
    tiles = got_ref.shape[1] // OWN - 1
    halves = loadings_ref.shape[1] // LANES

    def added(t):
        return sum(got_ref[h, t * OWN : (t + 1) * OWN, :].astype(F32) for h in range(4))

    library = jnp.sum(added(tiles), axis=1, keepdims=True)
    scores = jnp.zeros((OWN, loadings_ref.shape[1]), F32)
    rows_ref[...] = jnp.zeros_like(rows_ref)
    profile = []
    for t in range(tiles):
        normalized = jnp.log(1.0 + 10000.0 * added(t) / library).astype(BF16)
        rows_ref[pl.ds(t, OWN, stride=OWN), :] = normalized.astype(F32)
        profile.append(normalized)
    scores = jnp.dot(jnp.concatenate(profile, axis=1), loadings_ref[...], preferred_element_type=F32)
    for p, piece in enumerate(split3(scores)):
        for k in range(halves):
            at = tiles + p * halves + k
            rows_ref[pl.ds(at, OWN, stride=OWN), :] = piece[:, k * LANES : (k + 1) * LANES]
    for j in range(OWN):
        out_ref[j] = rows_ref[j * OWN : (j + 1) * OWN, :].astype(BF16)


def finish_kernel(got_ref, profile_ref, scores_ref):
    halves = scores_ref.shape[1] // LANES
    tiles = profile_ref.shape[1] // (got_ref.shape[0] * LANES)
    total = jnp.zeros((OWN, LANES), F32)
    for source in range(got_ref.shape[0]):
        block = got_ref[source].astype(F32)
        total += block
        for t in range(tiles):
            at = (source * tiles + t) * LANES
            profile_ref[:, at : at + LANES] = block[t : t + 1].astype(BF16)
    for k in range(halves):
        scores_ref[:, k * LANES : (k + 1) * LANES] = sum(
            total[tiles + p * halves + k : tiles + p * halves + k + 1] for p in range(3)
        )


def shards(labels, counts, library_size, loadings):
    cells, genes = counts.shape
    k = loadings.shape[1]
    tiles = genes // LANES
    width = 512
    sent = pl.pallas_call(
        sums_kernel,
        in_specs=[HBM, HBM, HBM],
        out_specs=VMEM,
        out_shape=pltpu.VMEM((8, tiles * 64 + OWN, LANES), BF16),
        scratch_shapes=[
            pltpu.VMEM((cells,), jnp.int32),
            pltpu.VMEM((cells,), jnp.int32),
            pltpu.VMEM((genes // width, cells, width), jnp.int32),
            pltpu.VMEM((G, cells), BF16),
            pltpu.VMEM((2 * LANES, cells), BF16),
            pltpu.VMEM((LANES, LANES), F32),
            pltpu.SemaphoreType.DMA((2,)),
            pltpu.SemaphoreType.DMA((genes // width,)),
        ],
        compiler_params=pltpu.CompilerParams(vmem_limit_bytes=LIMIT),
    )(*(pltpu.with_memory_space_constraint(array, pltpu.HBM) for array in (labels, library_size, counts)))
    got = lax.all_to_all(sent, "dp", 0, 0, tiled=True, axis_index_groups=FIRST)
    sent = pl.pallas_call(
        middle_kernel,
        in_specs=[VMEM],
        out_specs=VMEM,
        out_shape=jax.ShapeDtypeStruct((4, tiles * OWN + OWN, LANES), BF16),
        compiler_params=pltpu.CompilerParams(vmem_limit_bytes=LIMIT),
    )(got)
    got = lax.all_to_all(sent, "dp", 0, 0, tiled=True, axis_index_groups=SECOND)
    sent = pl.pallas_call(
        project_kernel,
        in_specs=[VMEM, VMEM],
        out_specs=VMEM,
        out_shape=jax.ShapeDtypeStruct((16, OWN, LANES), BF16),
        scratch_shapes=[pltpu.VMEM((16 * OWN, LANES), F32)],
        compiler_params=pltpu.CompilerParams(vmem_limit_bytes=LIMIT),
    )(got, loadings)
    got = lax.all_to_all(sent, "gene", 0, 0, tiled=True)
    return pl.pallas_call(
        finish_kernel,
        in_specs=[VMEM],
        out_specs=(VMEM, VMEM),
        out_shape=(
            jax.ShapeDtypeStruct((1, 16 * genes), BF16),
            jax.ShapeDtypeStruct((1, k), F32),
        ),
        compiler_params=pltpu.CompilerParams(vmem_limit_bytes=LIMIT),
    )(got)


def solution(mesh):
    placed = (P("dp"), P("dp", "gene"), P("dp"), P("gene", None))
    return jax.shard_map(
        shards,
        mesh=mesh,
        in_specs=placed,
        out_specs=(P(("dp", "gene"), None), P(("dp", "gene"), None)),
        check_vma=False,
    )
```

```python
import jax
import jax.numpy as jnp
from jax import lax
from jax.experimental import pallas as pl
from jax.experimental.pallas import tpu as pltpu
from jax.sharding import PartitionSpec as P

G = 512
F32 = jnp.float32
BF16 = jnp.bfloat16
LANES = 128
OWN = 16
Y_SETS = ((1, 2, 4, 7), (0, 3, 5, 6))
X_SETS = ((1, 2), (0, 3))
TILE, TILES = 4, 8


def member(z, core, y, x):
    return ((y + core) % 8 * 4 + (x + core) % 4) * 16 + z * 2 + core


FIRST = [
    [member(z, core, ys[h], xs[q]) for ys in Y_SETS for xs in X_SETS]
    for z in range(8)
    for core in range(2)
    for h in range(4)
    for q in range(2)
]
SECOND = [
    [member(z, core, ys[h], xs[q]) for h in range(4) for q in range(2)]
    for z in range(8)
    for core in range(2)
    for ys in Y_SETS
    for xs in X_SETS
]
VMEM = pl.BlockSpec(memory_space=pltpu.VMEM)
HBM = pl.BlockSpec(memory_space=pltpu.HBM)
LIMIT = 48 * 1024 * 1024


def split3(value):
    one = value.astype(BF16).astype(F32)
    two = (value - one).astype(BF16).astype(F32)
    return one, two, ((value - one) - two).astype(BF16).astype(F32)


def in_lanes(pieces, lane):
    return jnp.where(lane == 0, pieces[0], jnp.where(lane == 1, pieces[1], jnp.where(lane == 2, pieces[2], 0.0)))


def row_of(group, core):
    y = ((group >> 6) - core) & 7
    x = ((group >> 4) - core) & 3
    h, q = y >> 1, x >> 1
    y_set = (y ^ h ^ (h >> 1) ^ 1) & 1
    x_set = (x ^ q ^ 1) & 1
    return (((h * 2 + q) * 2 + y_set) * 2 + x_set) * OWN + (group & (OWN - 1))


def sums_kernel(
    labels_hbm,
    lib_hbm,
    counts_hbm,
    out_ref,
    labels_ref,
    lib_ref,
    counts_ref,
    members_ref,
    rows_ref,
    part_ref,
    tile_ref,
    small_sems,
    sems,
):
    blocks, cells, width = counts_ref.shape
    tiles = width // LANES
    span = tiles * TILES * OWN
    part = TILE * OWN
    chunk = 2 * part
    core = lax.axis_index("gene") & 1
    end = blocks * span

    def arriving(b):
        columns = pl.ds(pl.multiple_of(b * width, width), width)
        return pltpu.make_async_copy(counts_hbm.at[:, columns], counts_ref.at[b], sems.at[b])

    labels_copy = pltpu.make_async_copy(labels_hbm, labels_ref, small_sems.at[0])
    lib_copy = pltpu.make_async_copy(lib_hbm, lib_ref, small_sems.at[1])
    labels_copy.start()
    lib_copy.start()

    @pl.loop(0, blocks)
    def _(b):
        arriving(b).start()

    tile_ref[...] = jnp.zeros_like(tile_ref)
    labels_copy.wait()
    lib_copy.wait()
    rows_ref[...] = row_of(labels_ref[...].reshape(1, cells), core)
    size = lib_ref[...].reshape(1, cells)
    high = size // 256
    part_ref[:LANES] = jnp.broadcast_to(high.astype(F32), (LANES, cells)).astype(BF16)
    part_ref[LANES:] = jnp.broadcast_to((size - high * 256).astype(F32), (LANES, cells)).astype(BF16)

    @pl.loop(0, G // chunk)
    def _(i):
        at = pl.multiple_of(i * chunk, chunk)
        row = lax.broadcasted_iota(jnp.int32, (chunk, cells), 0) + at
        members = (row == rows_ref[...]).astype(F32).astype(BF16)
        members_ref[pl.ds(at, chunk), :] = members
        both = lax.dot_general(members, part_ref[...], (((1,), (1,)), ((), ())), preferred_element_type=F32)
        lane = lax.broadcasted_iota(jnp.int32, (chunk, LANES), 1)
        placed = in_lanes(split3(both[:, :LANES] * 256.0 + both[:, LANES:]), lane % 4)
        lane = lax.broadcasted_iota(jnp.int32, (part, LANES), 1) // 4
        tile = jnp.where(lane == 2 * i, placed[:part], tile_ref[...])
        tile_ref[...] = jnp.where(lane == 2 * i + 1, placed[part:], tile)

    out_ref[:, end:, :] = tile_ref[...].astype(BF16).reshape(TILE, OWN, LANES)

    @pl.loop(0, blocks)
    def _(b):
        arriving(b).wait()
        sums = jnp.dot(members_ref[...], counts_ref[b].astype(F32).astype(BF16), preferred_element_type=F32)
        sums = sums.astype(BF16)
        for t in range(tiles):
            for h in range(TILES):
                row = pl.multiple_of(b * span, span) + (t * TILES + h) * OWN
                block = sums[h * part : (h + 1) * part, t * LANES : (t + 1) * LANES]
                out_ref[:, pl.ds(row, OWN), :] = block.reshape(TILE, OWN, LANES)


def middle_kernel(got_ref, out_ref):
    tiles = (got_ref.shape[1] - OWN) // (TILES * OWN)

    def added(row):
        return sum(got_ref[m, row : row + OWN, :].astype(F32) for m in range(TILE))

    lane = lax.broadcasted_iota(jnp.int32, (OWN, LANES), 1)
    library = added(tiles * TILES * OWN)
    for h in range(TILES):
        for t in range(tiles):
            out_ref[h, t * OWN : (t + 1) * OWN, :] = added((t * TILES + h) * OWN).astype(BF16)
        mine = jnp.sum(jnp.where(lane // 4 == h, library, 0.0), axis=1, keepdims=True)
        out_ref[h, tiles * OWN :, :] = in_lanes(split3(mine), lane).astype(BF16)


def project_kernel(got_ref, loadings_ref, out_ref, rows_ref):
    tiles = got_ref.shape[1] // OWN - 1
    halves = loadings_ref.shape[1] // LANES

    def added(t):
        return sum(got_ref[h, t * OWN : (t + 1) * OWN, :].astype(F32) for h in range(TILES))

    library = jnp.sum(added(tiles), axis=1, keepdims=True)
    scores = jnp.zeros((OWN, loadings_ref.shape[1]), F32)
    rows_ref[...] = jnp.zeros_like(rows_ref)
    profile = []
    for t in range(tiles):
        normalized = jnp.log(1.0 + 10000.0 * added(t) / library).astype(BF16)
        rows_ref[pl.ds(t, OWN, stride=OWN), :] = normalized.astype(F32)
        profile.append(normalized)
    scores = jnp.dot(jnp.concatenate(profile, axis=1), loadings_ref[...], preferred_element_type=F32)
    for p, piece in enumerate(split3(scores)):
        for k in range(halves):
            at = tiles + p * halves + k
            rows_ref[pl.ds(at, OWN, stride=OWN), :] = piece[:, k * LANES : (k + 1) * LANES]
    for j in range(OWN):
        out_ref[j] = rows_ref[j * OWN : (j + 1) * OWN, :].astype(BF16)


def finish_kernel(got_ref, profile_ref, scores_ref):
    halves = scores_ref.shape[1] // LANES
    tiles = profile_ref.shape[1] // (got_ref.shape[0] * LANES)
    total = jnp.zeros((OWN, LANES), F32)
    for source in range(got_ref.shape[0]):
        block = got_ref[source].astype(F32)
        total += block
        for t in range(tiles):
            at = (source * tiles + t) * LANES
            profile_ref[:, at : at + LANES] = block[t : t + 1].astype(BF16)
    for k in range(halves):
        scores_ref[:, k * LANES : (k + 1) * LANES] = sum(
            total[tiles + p * halves + k : tiles + p * halves + k + 1] for p in range(3)
        )


def shards(labels, counts, library_size, loadings):
    cells, genes = counts.shape
    k = loadings.shape[1]
    tiles = genes // LANES
    width = 512
    sent = pl.pallas_call(
        sums_kernel,
        in_specs=[HBM, HBM, HBM],
        out_specs=VMEM,
        out_shape=pltpu.VMEM((TILE, tiles * TILES * OWN + OWN, LANES), BF16),
        scratch_shapes=[
            pltpu.VMEM((cells,), jnp.int32),
            pltpu.VMEM((cells,), jnp.int32),
            pltpu.VMEM((genes // width, cells, width), jnp.int32),
            pltpu.VMEM((G, cells), BF16),
            pltpu.VMEM((1, cells), jnp.int32),
            pltpu.VMEM((2 * LANES, cells), BF16),
            pltpu.VMEM((TILE * OWN, LANES), F32),
            pltpu.SemaphoreType.DMA((2,)),
            pltpu.SemaphoreType.DMA((genes // width,)),
        ],
        compiler_params=pltpu.CompilerParams(vmem_limit_bytes=LIMIT),
    )(*(pltpu.with_memory_space_constraint(array, pltpu.HBM) for array in (labels, library_size, counts)))
    got = lax.all_to_all(sent, ("dp", "gene"), 0, 0, tiled=True, axis_index_groups=FIRST)
    sent = pl.pallas_call(
        middle_kernel,
        in_specs=[VMEM],
        out_specs=VMEM,
        out_shape=jax.ShapeDtypeStruct((TILES, tiles * OWN + OWN, LANES), BF16),
        compiler_params=pltpu.CompilerParams(vmem_limit_bytes=LIMIT),
    )(got)
    got = lax.all_to_all(sent, ("dp", "gene"), 0, 0, tiled=True, axis_index_groups=SECOND)
    sent = pl.pallas_call(
        project_kernel,
        in_specs=[VMEM, VMEM],
        out_specs=VMEM,
        out_shape=jax.ShapeDtypeStruct((16, OWN, LANES), BF16),
        scratch_shapes=[pltpu.VMEM((16 * OWN, LANES), F32)],
        compiler_params=pltpu.CompilerParams(vmem_limit_bytes=LIMIT),
    )(got, loadings)
    got = lax.all_to_all(sent, "gene", 0, 0, tiled=True)
    return pl.pallas_call(
        finish_kernel,
        in_specs=[VMEM],
        out_specs=(VMEM, VMEM),
        out_shape=(
            jax.ShapeDtypeStruct((1, 16 * genes), BF16),
            jax.ShapeDtypeStruct((1, k), F32),
        ),
        compiler_params=pltpu.CompilerParams(vmem_limit_bytes=LIMIT),
    )(got)


def solution(mesh):
    placed = (P("dp"), P("dp", "gene"), P("dp"), P("gene", None))
    return jax.shard_map(
        shards,
        mesh=mesh,
        in_specs=placed,
        out_specs=(P(("dp", "gene"), None), P(("dp", "gene"), None)),
        check_vma=False,
    )
```

```python
import jax
import jax.numpy as jnp
from jax import lax
from jax.experimental import pallas as pl
from jax.experimental.pallas import tpu as pltpu
from jax.sharding import PartitionSpec as P

G = 512
F32 = jnp.float32
BF16 = jnp.bfloat16
LANES = 128
OWN = 16
Y_SETS = ((1, 2, 4, 7), (0, 3, 5, 6))
X_SETS = ((1, 2), (0, 3))
TILE, TILES = 4, 8


def member(z, core, y, x):
    return ((y + core) % 8 * 4 + (x + core) % 4) * 16 + z * 2 + core


FIRST = [
    [member(z, core, ys[h], xs[q]) for ys in Y_SETS for xs in X_SETS]
    for z in range(8)
    for core in range(2)
    for h in range(4)
    for q in range(2)
]
SECOND = [
    [member(z, core, ys[h], xs[q]) for h in range(4) for q in range(2)]
    for z in range(8)
    for core in range(2)
    for ys in Y_SETS
    for xs in X_SETS
]
VMEM = pl.BlockSpec(memory_space=pltpu.VMEM)
HBM = pl.BlockSpec(memory_space=pltpu.HBM)
LIMIT = 48 * 1024 * 1024


def split3(value):
    one = value.astype(BF16).astype(F32)
    two = (value - one).astype(BF16).astype(F32)
    return one, two, ((value - one) - two).astype(BF16).astype(F32)


def in_lanes(pieces, lane):
    return jnp.where(lane == 0, pieces[0], jnp.where(lane == 1, pieces[1], jnp.where(lane == 2, pieces[2], 0.0)))


def row_of(group, core):
    y = ((group >> 6) - core) & 7
    x = ((group >> 4) - core) & 3
    h, q = y >> 1, x >> 1
    y_set = (y ^ h ^ (h >> 1) ^ 1) & 1
    x_set = (x ^ q ^ 1) & 1
    return (((h * 2 + q) * 2 + y_set) * 2 + x_set) * OWN + (group & (OWN - 1))


def sums_kernel(
    labels_hbm,
    lib_hbm,
    counts_hbm,
    out_ref,
    labels_ref,
    lib_ref,
    counts_ref,
    members_ref,
    rows_ref,
    small_sems,
    sems,
):
    blocks, cells, width = counts_ref.shape
    tiles = width // LANES
    span = tiles * TILES * OWN
    part = TILE * OWN
    chunk = 2 * part
    core = lax.axis_index("gene") & 1
    end = blocks * span

    def arriving(b):
        columns = pl.ds(pl.multiple_of(b * width, width), width)
        return pltpu.make_async_copy(counts_hbm.at[:, columns], counts_ref.at[b], sems.at[b])

    labels_copy = pltpu.make_async_copy(labels_hbm, labels_ref, small_sems.at[0])
    lib_copy = pltpu.make_async_copy(lib_hbm, lib_ref, small_sems.at[1])
    labels_copy.start()
    lib_copy.start()

    @pl.loop(0, blocks)
    def _(b):
        arriving(b).start()

    labels_copy.wait()
    rows_ref[...] = row_of(labels_ref[...].reshape(1, cells), core)

    @pl.loop(0, G // chunk)
    def _(i):
        at = pl.multiple_of(i * chunk, chunk)
        row = lax.broadcasted_iota(jnp.int32, (chunk, cells), 0) + at
        members_ref[pl.ds(at, chunk), :] = (row == rows_ref[...]).astype(F32).astype(BF16)

    lib_copy.wait()
    size = lib_ref[...].reshape(1, cells)
    low = size & 255
    lane = lax.broadcasted_iota(jnp.int32, (LANES, cells), 0)
    sizes = jnp.where(lane & 4 == 0, size - low, low).astype(F32).astype(BF16)
    total = lax.dot_general(members_ref[...], sizes, (((1,), (1,)), ((), ())), preferred_element_type=F32)
    placed = in_lanes(split3(total), lax.broadcasted_iota(jnp.int32, (G, LANES), 1) & 3)
    lane = lax.broadcasted_iota(jnp.int32, (part, LANES), 1) >> 3
    tile = jnp.zeros((part, LANES), F32)
    for h in range(TILES):
        tile = jnp.where(lane == h, placed[h * part : (h + 1) * part], tile)
    out_ref[:, end:, :] = tile.astype(BF16).reshape(TILE, OWN, LANES)

    @pl.loop(0, blocks)
    def _(b):
        arriving(b).wait()
        sums = jnp.dot(members_ref[...], counts_ref[b].astype(F32).astype(BF16), preferred_element_type=F32)
        sums = sums.astype(BF16)
        for t in range(tiles):
            for h in range(TILES):
                row = pl.multiple_of(b * span, span) + (t * TILES + h) * OWN
                block = sums[h * part : (h + 1) * part, t * LANES : (t + 1) * LANES]
                out_ref[:, pl.ds(row, OWN), :] = block.reshape(TILE, OWN, LANES)


def middle_kernel(got_ref, out_ref):
    tiles = (got_ref.shape[1] - OWN) // (TILES * OWN)

    def added(row):
        return sum(got_ref[m, row : row + OWN, :].astype(F32) for m in range(TILE))

    lane = lax.broadcasted_iota(jnp.int32, (OWN, LANES), 1)
    library = added(tiles * TILES * OWN)
    for h in range(TILES):
        for t in range(tiles):
            out_ref[h, t * OWN : (t + 1) * OWN, :] = added((t * TILES + h) * OWN).astype(BF16)
        mine = jnp.sum(jnp.where(lane >> 3 == h, library, 0.0), axis=1, keepdims=True)
        out_ref[h, tiles * OWN :, :] = in_lanes(split3(mine), lane).astype(BF16)


def project_kernel(got_ref, loadings_ref, out_ref, rows_ref):
    tiles = got_ref.shape[1] // OWN - 1
    halves = loadings_ref.shape[1] // LANES

    def added(t):
        return sum(got_ref[h, t * OWN : (t + 1) * OWN, :].astype(F32) for h in range(TILES))

    library = jnp.sum(added(tiles), axis=1, keepdims=True)
    rows_ref[...] = jnp.zeros_like(rows_ref)
    profile = []
    for t in range(tiles):
        normalized = jnp.log(1.0 + 10000.0 * added(t) / library).astype(BF16)
        rows_ref[pl.ds(t, OWN, stride=OWN), :] = normalized.astype(F32)
        profile.append(normalized)
    scores = jnp.dot(jnp.concatenate(profile, axis=1), loadings_ref[...], preferred_element_type=F32)
    for p, piece in enumerate(split3(scores)):
        for k in range(halves):
            at = tiles + p * halves + k
            rows_ref[pl.ds(at, OWN, stride=OWN), :] = piece[:, k * LANES : (k + 1) * LANES]
    for j in range(OWN):
        out_ref[j] = rows_ref[j * OWN : (j + 1) * OWN, :].astype(BF16)


def finish_kernel(got_ref, profile_ref, scores_ref):
    halves = scores_ref.shape[1] // LANES
    tiles = profile_ref.shape[1] // (got_ref.shape[0] * LANES)
    total = jnp.zeros((OWN, LANES), F32)
    for source in range(got_ref.shape[0]):
        block = got_ref[source].astype(F32)
        total += block
        for t in range(tiles):
            at = (source * tiles + t) * LANES
            profile_ref[:, at : at + LANES] = block[t : t + 1].astype(BF16)
    for k in range(halves):
        scores_ref[:, k * LANES : (k + 1) * LANES] = sum(
            total[tiles + p * halves + k : tiles + p * halves + k + 1] for p in range(3)
        )


def local_sums(labels, library_size, counts):
    cells, genes = counts.shape
    tiles = genes // LANES
    width = 512
    return pl.pallas_call(
        sums_kernel,
        in_specs=[HBM, HBM, HBM],
        out_specs=VMEM,
        out_shape=pltpu.VMEM((TILE, tiles * TILES * OWN + OWN, LANES), BF16),
        scratch_shapes=[
            pltpu.VMEM((cells,), jnp.int32),
            pltpu.VMEM((cells,), jnp.int32),
            pltpu.VMEM((genes // width, cells, width), jnp.int32),
            pltpu.VMEM((G, cells), BF16),
            pltpu.VMEM((1, cells), jnp.int32),
            pltpu.SemaphoreType.DMA((2,)),
            pltpu.SemaphoreType.DMA((genes // width,)),
        ],
        compiler_params=pltpu.CompilerParams(vmem_limit_bytes=LIMIT),
    )(*(pltpu.with_memory_space_constraint(array, pltpu.HBM) for array in (labels, library_size, counts)))


def shards(labels, counts, library_size, loadings):
    cells, genes = counts.shape
    k = loadings.shape[1]
    tiles = genes // LANES
    sent = local_sums(labels, library_size, counts)
    got = lax.all_to_all(sent, ("dp", "gene"), 0, 0, tiled=True, axis_index_groups=FIRST)
    sent = pl.pallas_call(
        middle_kernel,
        in_specs=[VMEM],
        out_specs=VMEM,
        out_shape=jax.ShapeDtypeStruct((TILES, tiles * OWN + OWN, LANES), BF16),
        compiler_params=pltpu.CompilerParams(vmem_limit_bytes=LIMIT),
    )(got)
    got = lax.all_to_all(sent, ("dp", "gene"), 0, 0, tiled=True, axis_index_groups=SECOND)
    sent = pl.pallas_call(
        project_kernel,
        in_specs=[VMEM, VMEM],
        out_specs=VMEM,
        out_shape=jax.ShapeDtypeStruct((16, OWN, LANES), BF16),
        scratch_shapes=[pltpu.VMEM((16 * OWN, LANES), F32)],
        compiler_params=pltpu.CompilerParams(vmem_limit_bytes=LIMIT),
    )(got, loadings)
    got = lax.all_to_all(sent, "gene", 0, 0, tiled=True)
    return pl.pallas_call(
        finish_kernel,
        in_specs=[VMEM],
        out_specs=(VMEM, VMEM),
        out_shape=(
            jax.ShapeDtypeStruct((1, 16 * genes), BF16),
            jax.ShapeDtypeStruct((1, k), F32),
        ),
        compiler_params=pltpu.CompilerParams(vmem_limit_bytes=LIMIT),
    )(got)


def solution(mesh):
    placed = (P("dp"), P("dp", "gene"), P("dp"), P("gene", None))
    return jax.shard_map(
        shards,
        mesh=mesh,
        in_specs=placed,
        out_specs=(P(("dp", "gene"), None), P(("dp", "gene"), None)),
        check_vma=False,
    )
```

```python
import jax
import jax.numpy as jnp
from jax import lax
from jax.experimental import pallas as pl
from jax.experimental.pallas import tpu as pltpu
from jax.sharding import PartitionSpec as P

G = 512
F32 = jnp.float32
BF16 = jnp.bfloat16
LANES = 128
OWN = 16
Y_SETS = ((1, 2, 4, 7), (0, 3, 5, 6))
X_SETS = ((1, 2), (0, 3))
TILE, TILES = 4, 8


def origin(core):
    return 4 + 3 * core, 3 * core


def member(z, core, y, x):
    y_from, x_from = origin(core)
    return ((y + y_from) % 8 * 4 + (x + x_from) % 4) * 16 + z * 2 + core


FIRST = [
    [member(z, core, ys[h], xs[q]) for ys in Y_SETS for xs in X_SETS]
    for z in range(8)
    for core in range(2)
    for h in range(4)
    for q in range(2)
]
SECOND = [
    [member(z, core, ys[h], xs[q]) for h in range(4) for q in range(2)]
    for z in range(8)
    for core in range(2)
    for ys in Y_SETS
    for xs in X_SETS
]
VMEM = pl.BlockSpec(memory_space=pltpu.VMEM)
HBM = pl.BlockSpec(memory_space=pltpu.HBM)
LIMIT = 48 * 1024 * 1024


def split3(value):
    one = value.astype(BF16).astype(F32)
    two = (value - one).astype(BF16).astype(F32)
    return one, two, ((value - one) - two).astype(BF16).astype(F32)


def in_lanes(pieces, lane):
    return jnp.where(lane == 0, pieces[0], jnp.where(lane == 1, pieces[1], jnp.where(lane == 2, pieces[2], 0.0)))


def row_of(group, core):
    y_from, x_from = origin(core)
    y = ((group >> 6) - y_from) & 7
    x = ((group >> 4) - x_from) & 3
    h, q = y >> 1, x >> 1
    y_set = (y ^ h ^ (h >> 1) ^ 1) & 1
    x_set = (x ^ q ^ 1) & 1
    return (((h * 2 + q) * 2 + y_set) * 2 + x_set) * OWN + (group & (OWN - 1))


def sums_kernel(
    labels_hbm,
    lib_hbm,
    counts_hbm,
    out_ref,
    labels_ref,
    lib_ref,
    counts_ref,
    members_ref,
    rows_ref,
    small_sems,
    sems,
):
    blocks, cells, width = counts_ref.shape
    tiles = width // LANES
    span = tiles * TILES * OWN
    part = TILE * OWN
    chunk = 2 * part
    core = lax.axis_index("gene") & 1
    end = blocks * span

    def arriving(b):
        columns = pl.ds(pl.multiple_of(b * width, width), width)
        return pltpu.make_async_copy(counts_hbm.at[:, columns], counts_ref.at[b], sems.at[b])

    labels_copy = pltpu.make_async_copy(labels_hbm, labels_ref, small_sems.at[0])
    lib_copy = pltpu.make_async_copy(lib_hbm, lib_ref, small_sems.at[1])
    labels_copy.start()
    lib_copy.start()

    @pl.loop(0, blocks)
    def _(b):
        arriving(b).start()

    labels_copy.wait()
    rows_ref[...] = row_of(labels_ref[...].reshape(1, cells), core)

    @pl.loop(0, G // chunk)
    def _(i):
        at = pl.multiple_of(i * chunk, chunk)
        row = lax.broadcasted_iota(jnp.int32, (chunk, cells), 0) + at
        members_ref[pl.ds(at, chunk), :] = (row == rows_ref[...]).astype(F32).astype(BF16)

    lib_copy.wait()
    size = lib_ref[...].reshape(1, cells)
    low = size & 255
    lane = lax.broadcasted_iota(jnp.int32, (LANES, cells), 0)
    sizes = jnp.where(lane & 4 == 0, size - low, low).astype(F32).astype(BF16)
    total = lax.dot_general(members_ref[...], sizes, (((1,), (1,)), ((), ())), preferred_element_type=F32)
    placed = in_lanes(split3(total), lax.broadcasted_iota(jnp.int32, (G, LANES), 1) & 3)
    lane = lax.broadcasted_iota(jnp.int32, (part, LANES), 1) >> 3
    tile = jnp.zeros((part, LANES), F32)
    for h in range(TILES):
        tile = jnp.where(lane == h, placed[h * part : (h + 1) * part], tile)
    out_ref[:, end:, :] = tile.astype(BF16).reshape(TILE, OWN, LANES)

    @pl.loop(0, blocks)
    def _(b):
        arriving(b).wait()
        sums = jnp.dot(members_ref[...], counts_ref[b].astype(F32).astype(BF16), preferred_element_type=F32)
        sums = sums.astype(BF16)
        for t in range(tiles):
            for h in range(TILES):
                row = pl.multiple_of(b * span, span) + (t * TILES + h) * OWN
                block = sums[h * part : (h + 1) * part, t * LANES : (t + 1) * LANES]
                out_ref[:, pl.ds(row, OWN), :] = block.reshape(TILE, OWN, LANES)


def middle_kernel(got_ref, out_ref):
    tiles = (got_ref.shape[1] - OWN) // (TILES * OWN)

    def added(row):
        return sum(got_ref[m, row : row + OWN, :].astype(F32) for m in range(TILE))

    lane = lax.broadcasted_iota(jnp.int32, (OWN, LANES), 1)
    library = added(tiles * TILES * OWN)
    for h in range(TILES):
        for t in range(tiles):
            out_ref[h, t * OWN : (t + 1) * OWN, :] = added((t * TILES + h) * OWN).astype(BF16)
        mine = jnp.sum(jnp.where(lane >> 3 == h, library, 0.0), axis=1, keepdims=True)
        out_ref[h, tiles * OWN :, :] = in_lanes(split3(mine), lane).astype(BF16)


def project_kernel(got_ref, loadings_ref, out_ref, rows_ref):
    tiles = got_ref.shape[1] // OWN - 1
    halves = loadings_ref.shape[1] // LANES

    def added(t):
        return sum(got_ref[h, t * OWN : (t + 1) * OWN, :].astype(F32) for h in range(TILES))

    library = jnp.sum(added(tiles), axis=1, keepdims=True)
    rows_ref[...] = jnp.zeros_like(rows_ref)
    profile = []
    for t in range(tiles):
        normalized = jnp.log(1.0 + 10000.0 * added(t) / library).astype(BF16)
        rows_ref[pl.ds(t, OWN, stride=OWN), :] = normalized.astype(F32)
        profile.append(normalized)
    scores = jnp.dot(jnp.concatenate(profile, axis=1), loadings_ref[...], preferred_element_type=F32)
    for p, piece in enumerate(split3(scores)):
        for k in range(halves):
            at = tiles + p * halves + k
            rows_ref[pl.ds(at, OWN, stride=OWN), :] = piece[:, k * LANES : (k + 1) * LANES]
    for j in range(OWN):
        out_ref[j] = rows_ref[j * OWN : (j + 1) * OWN, :].astype(BF16)


def finish_kernel(got_ref, profile_ref, scores_ref):
    halves = scores_ref.shape[1] // LANES
    tiles = profile_ref.shape[1] // (got_ref.shape[0] * LANES)
    total = jnp.zeros((OWN, LANES), F32)
    for source in range(got_ref.shape[0]):
        block = got_ref[source].astype(F32)
        total += block
        for t in range(tiles):
            at = (source * tiles + t) * LANES
            profile_ref[:, at : at + LANES] = block[t : t + 1].astype(BF16)
    for k in range(halves):
        scores_ref[:, k * LANES : (k + 1) * LANES] = sum(
            total[tiles + p * halves + k : tiles + p * halves + k + 1] for p in range(3)
        )


def local_sums(labels, library_size, counts):
    cells, genes = counts.shape
    tiles = genes // LANES
    width = 512
    return pl.pallas_call(
        sums_kernel,
        in_specs=[HBM, HBM, HBM],
        out_specs=VMEM,
        out_shape=pltpu.VMEM((TILE, tiles * TILES * OWN + OWN, LANES), BF16),
        scratch_shapes=[
            pltpu.VMEM((cells,), jnp.int32),
            pltpu.VMEM((cells,), jnp.int32),
            pltpu.VMEM((genes // width, cells, width), jnp.int32),
            pltpu.VMEM((G, cells), BF16),
            pltpu.VMEM((1, cells), jnp.int32),
            pltpu.SemaphoreType.DMA((2,)),
            pltpu.SemaphoreType.DMA((genes // width,)),
        ],
        compiler_params=pltpu.CompilerParams(vmem_limit_bytes=LIMIT),
    )(*(pltpu.with_memory_space_constraint(array, pltpu.HBM) for array in (labels, library_size, counts)))


def shards(labels, counts, library_size, loadings):
    cells, genes = counts.shape
    k = loadings.shape[1]
    tiles = genes // LANES
    sent = local_sums(labels, library_size, counts)
    got = lax.all_to_all(sent, ("dp", "gene"), 0, 0, tiled=True, axis_index_groups=FIRST)
    sent = pl.pallas_call(
        middle_kernel,
        in_specs=[VMEM],
        out_specs=VMEM,
        out_shape=jax.ShapeDtypeStruct((TILES, tiles * OWN + OWN, LANES), BF16),
        compiler_params=pltpu.CompilerParams(vmem_limit_bytes=LIMIT),
    )(got)
    got = lax.all_to_all(sent, ("dp", "gene"), 0, 0, tiled=True, axis_index_groups=SECOND)
    sent = pl.pallas_call(
        project_kernel,
        in_specs=[VMEM, VMEM],
        out_specs=VMEM,
        out_shape=jax.ShapeDtypeStruct((16, OWN, LANES), BF16),
        scratch_shapes=[pltpu.VMEM((16 * OWN, LANES), F32)],
        compiler_params=pltpu.CompilerParams(vmem_limit_bytes=LIMIT),
    )(got, loadings)
    got = lax.all_to_all(sent, "gene", 0, 0, tiled=True)
    return pl.pallas_call(
        finish_kernel,
        in_specs=[VMEM],
        out_specs=(VMEM, VMEM),
        out_shape=(
            jax.ShapeDtypeStruct((1, 16 * genes), BF16),
            jax.ShapeDtypeStruct((1, k), F32),
        ),
        compiler_params=pltpu.CompilerParams(vmem_limit_bytes=LIMIT),
    )(got)


def solution(mesh):
    placed = (P("dp"), P("dp", "gene"), P("dp"), P("gene", None))
    return jax.shard_map(
        shards,
        mesh=mesh,
        in_specs=placed,
        out_specs=(P(("dp", "gene"), None), P(("dp", "gene"), None)),
        check_vma=False,
    )
```

```python
import jax
import jax.numpy as jnp
from jax import lax
from jax.experimental import pallas as pl
from jax.experimental.pallas import tpu as pltpu
from jax.sharding import PartitionSpec as P

G = 512
F32 = jnp.float32
BF16 = jnp.bfloat16
LANES = 128
OWN = 16
Y_SETS = ((1, 2, 4, 7), (0, 3, 5, 6))
X_SETS = ((1, 2), (0, 3))
TILE, TILES = 4, 8


def origin(core):
    return 4 + 3 * core, 2 - core


def member(z, core, y, x):
    y_from, x_from = origin(core)
    return ((y + y_from) % 8 * 4 + (x + x_from) % 4) * 16 + z * 2 + core


FIRST = [
    [member(z, core, ys[h], xs[q]) for ys in Y_SETS for xs in X_SETS]
    for z in range(8)
    for core in range(2)
    for h in range(4)
    for q in range(2)
]
SECOND = [
    [member(z, core, ys[h], xs[q]) for h in range(4) for q in range(2)]
    for z in range(8)
    for core in range(2)
    for ys in Y_SETS
    for xs in X_SETS
]
VMEM = pl.BlockSpec(memory_space=pltpu.VMEM)
HBM = pl.BlockSpec(memory_space=pltpu.HBM)
LIMIT = 48 * 1024 * 1024


def split3(value):
    one = value.astype(BF16).astype(F32)
    two = (value - one).astype(BF16).astype(F32)
    return one, two, ((value - one) - two).astype(BF16).astype(F32)


def in_lanes(pieces, lane):
    return jnp.where(lane == 0, pieces[0], jnp.where(lane == 1, pieces[1], jnp.where(lane == 2, pieces[2], 0.0)))


def row_of(group, core):
    y_from, x_from = origin(core)
    y = ((group >> 6) - y_from) & 7
    x = ((group >> 4) - x_from) & 3
    h, q = y >> 1, x >> 1
    y_set = (y ^ h ^ (h >> 1) ^ 1) & 1
    x_set = (x ^ q ^ 1) & 1
    return (((h * 2 + q) * 2 + y_set) * 2 + x_set) * OWN + (group & (OWN - 1))


def sums_kernel(
    labels_hbm,
    lib_hbm,
    counts_hbm,
    out_ref,
    labels_ref,
    lib_ref,
    counts_ref,
    members_ref,
    rows_ref,
    small_sems,
    sems,
):
    blocks, cells, width = counts_ref.shape
    tiles = width // LANES
    span = tiles * TILES * OWN
    part = TILE * OWN
    chunk = 2 * part
    core = lax.axis_index("gene") & 1
    end = blocks * span

    def arriving(b):
        columns = pl.ds(pl.multiple_of(b * width, width), width)
        return pltpu.make_async_copy(counts_hbm.at[:, columns], counts_ref.at[b], sems.at[b])

    labels_copy = pltpu.make_async_copy(labels_hbm, labels_ref, small_sems.at[0])
    lib_copy = pltpu.make_async_copy(lib_hbm, lib_ref, small_sems.at[1])
    labels_copy.start()
    lib_copy.start()

    @pl.loop(0, blocks)
    def _(b):
        arriving(b).start()

    labels_copy.wait()
    rows_ref[...] = row_of(labels_ref[...].reshape(1, cells), core)

    @pl.loop(0, G // chunk)
    def _(i):
        at = pl.multiple_of(i * chunk, chunk)
        row = lax.broadcasted_iota(jnp.int32, (chunk, cells), 0) + at
        members_ref[pl.ds(at, chunk), :] = (row == rows_ref[...]).astype(F32).astype(BF16)

    lib_copy.wait()
    size = lib_ref[...].reshape(1, cells)
    low = size & 255
    lane = lax.broadcasted_iota(jnp.int32, (LANES, cells), 0)
    sizes = jnp.where(lane & 4 == 0, size - low, low).astype(F32).astype(BF16)
    total = lax.dot_general(members_ref[...], sizes, (((1,), (1,)), ((), ())), preferred_element_type=F32)
    placed = in_lanes(split3(total), lax.broadcasted_iota(jnp.int32, (G, LANES), 1) & 3)
    lane = lax.broadcasted_iota(jnp.int32, (part, LANES), 1) >> 3
    tile = jnp.zeros((part, LANES), F32)
    for h in range(TILES):
        tile = jnp.where(lane == h, placed[h * part : (h + 1) * part], tile)
    out_ref[:, end:, :] = tile.astype(BF16).reshape(TILE, OWN, LANES)

    @pl.loop(0, blocks)
    def _(b):
        arriving(b).wait()
        sums = jnp.dot(members_ref[...], counts_ref[b].astype(F32).astype(BF16), preferred_element_type=F32)
        sums = sums.astype(BF16)
        for t in range(tiles):
            for h in range(TILES):
                row = pl.multiple_of(b * span, span) + (t * TILES + h) * OWN
                block = sums[h * part : (h + 1) * part, t * LANES : (t + 1) * LANES]
                out_ref[:, pl.ds(row, OWN), :] = block.reshape(TILE, OWN, LANES)


def middle_kernel(got_ref, out_ref):
    tiles = (got_ref.shape[1] - OWN) // (TILES * OWN)

    def added(row):
        return sum(got_ref[m, row : row + OWN, :].astype(F32) for m in range(TILE))

    lane = lax.broadcasted_iota(jnp.int32, (OWN, LANES), 1)
    library = added(tiles * TILES * OWN)
    for h in range(TILES):
        for t in range(tiles):
            out_ref[h, t * OWN : (t + 1) * OWN, :] = added((t * TILES + h) * OWN).astype(BF16)
        mine = jnp.sum(jnp.where(lane >> 3 == h, library, 0.0), axis=1, keepdims=True)
        out_ref[h, tiles * OWN :, :] = in_lanes(split3(mine), lane).astype(BF16)


def project_kernel(got_ref, loadings_ref, out_ref, rows_ref):
    tiles = got_ref.shape[1] // OWN - 1
    halves = loadings_ref.shape[1] // LANES

    def added(t):
        return sum(got_ref[h, t * OWN : (t + 1) * OWN, :].astype(F32) for h in range(TILES))

    library = jnp.sum(added(tiles), axis=1, keepdims=True)
    rows_ref[...] = jnp.zeros_like(rows_ref)
    profile = []
    for t in range(tiles):
        normalized = jnp.log(1.0 + 10000.0 * added(t) / library).astype(BF16)
        rows_ref[pl.ds(t, OWN, stride=OWN), :] = normalized.astype(F32)
        profile.append(normalized)
    scores = jnp.dot(jnp.concatenate(profile, axis=1), loadings_ref[...], preferred_element_type=F32)
    for p, piece in enumerate(split3(scores)):
        for k in range(halves):
            at = tiles + p * halves + k
            rows_ref[pl.ds(at, OWN, stride=OWN), :] = piece[:, k * LANES : (k + 1) * LANES]
    for j in range(OWN):
        out_ref[j] = rows_ref[j * OWN : (j + 1) * OWN, :].astype(BF16)


def finish_kernel(got_ref, profile_ref, scores_ref):
    halves = scores_ref.shape[1] // LANES
    tiles = profile_ref.shape[1] // (got_ref.shape[0] * LANES)
    total = jnp.zeros((OWN, LANES), F32)
    for source in range(got_ref.shape[0]):
        block = got_ref[source].astype(F32)
        total += block
        for t in range(tiles):
            at = (source * tiles + t) * LANES
            profile_ref[:, at : at + LANES] = block[t : t + 1].astype(BF16)
    for k in range(halves):
        scores_ref[:, k * LANES : (k + 1) * LANES] = sum(
            total[tiles + p * halves + k : tiles + p * halves + k + 1] for p in range(3)
        )


def local_sums(labels, library_size, counts):
    cells, genes = counts.shape
    tiles = genes // LANES
    width = 512
    return pl.pallas_call(
        sums_kernel,
        in_specs=[HBM, HBM, HBM],
        out_specs=VMEM,
        out_shape=pltpu.VMEM((TILE, tiles * TILES * OWN + OWN, LANES), BF16),
        scratch_shapes=[
            pltpu.VMEM((cells,), jnp.int32),
            pltpu.VMEM((cells,), jnp.int32),
            pltpu.VMEM((genes // width, cells, width), jnp.int32),
            pltpu.VMEM((G, cells), BF16),
            pltpu.VMEM((1, cells), jnp.int32),
            pltpu.SemaphoreType.DMA((2,)),
            pltpu.SemaphoreType.DMA((genes // width,)),
        ],
        compiler_params=pltpu.CompilerParams(vmem_limit_bytes=LIMIT),
    )(*(pltpu.with_memory_space_constraint(array, pltpu.HBM) for array in (labels, library_size, counts)))


def shards(labels, counts, library_size, loadings):
    cells, genes = counts.shape
    k = loadings.shape[1]
    tiles = genes // LANES
    sent = local_sums(labels, library_size, counts)
    got = lax.all_to_all(sent, ("dp", "gene"), 0, 0, tiled=True, axis_index_groups=FIRST)
    sent = pl.pallas_call(
        middle_kernel,
        in_specs=[VMEM],
        out_specs=VMEM,
        out_shape=jax.ShapeDtypeStruct((TILES, tiles * OWN + OWN, LANES), BF16),
        compiler_params=pltpu.CompilerParams(vmem_limit_bytes=LIMIT),
    )(got)
    got = lax.all_to_all(sent, ("dp", "gene"), 0, 0, tiled=True, axis_index_groups=SECOND)
    sent = pl.pallas_call(
        project_kernel,
        in_specs=[VMEM, VMEM],
        out_specs=VMEM,
        out_shape=jax.ShapeDtypeStruct((16, OWN, LANES), BF16),
        scratch_shapes=[pltpu.VMEM((16 * OWN, LANES), F32)],
        compiler_params=pltpu.CompilerParams(vmem_limit_bytes=LIMIT),
    )(got, loadings)
    got = lax.all_to_all(sent, "gene", 0, 0, tiled=True)
    return pl.pallas_call(
        finish_kernel,
        in_specs=[VMEM],
        out_specs=(VMEM, VMEM),
        out_shape=(
            jax.ShapeDtypeStruct((1, 16 * genes), BF16),
            jax.ShapeDtypeStruct((1, k), F32),
        ),
        compiler_params=pltpu.CompilerParams(vmem_limit_bytes=LIMIT),
    )(got)


def solution(mesh):
    placed = (P("dp"), P("dp", "gene"), P("dp"), P("gene", None))
    return jax.shard_map(
        shards,
        mesh=mesh,
        in_specs=placed,
        out_specs=(P(("dp", "gene"), None), P(("dp", "gene"), None)),
        check_vma=False,
    )
```

```python
import jax
import jax.numpy as jnp
from jax import lax
from jax.experimental import pallas as pl
from jax.experimental.pallas import tpu as pltpu
from jax.sharding import PartitionSpec as P

G = 512
F32 = jnp.float32
BF16 = jnp.bfloat16
LANES = 128
HALF = 8
OWN = 16
Y_SETS = ((1, 2, 4, 7), (0, 3, 5, 6))
X_SETS = ((1, 2), (0, 3))
TILE, TILES = 4, 8


def origin(core):
    return 4 + 3 * core, 2 - core


def member(z, core, y, x):
    y_from, x_from = origin(core)
    return ((y + y_from) % 8 * 4 + (x + x_from) % 4) * 16 + z * 2 + core


FIRST = [
    [member(z, core, ys[h], xs[q]) for ys in Y_SETS for xs in X_SETS]
    for z in range(8)
    for core in range(2)
    for h in range(4)
    for q in range(2)
]
SECOND = [
    [member(z, core, ys[h], xs[q]) for h in range(4) for q in range(2)]
    for z in range(8)
    for core in range(2)
    for ys in Y_SETS
    for xs in X_SETS
]
VMEM = pl.BlockSpec(memory_space=pltpu.VMEM)
HBM = pl.BlockSpec(memory_space=pltpu.HBM)
LIMIT = 48 * 1024 * 1024


def split3(value):
    one = value.astype(BF16).astype(F32)
    two = (value - one).astype(BF16).astype(F32)
    return one, two, ((value - one) - two).astype(BF16).astype(F32)


def in_lanes(pieces, lane):
    return jnp.where(lane == 0, pieces[0], jnp.where(lane == 1, pieces[1], jnp.where(lane == 2, pieces[2], 0.0)))


def row_of(group, core):
    y_from, x_from = origin(core)
    y = ((group >> 6) - y_from) & 7
    x = ((group >> 4) - x_from) & 3
    h, q = y >> 1, x >> 1
    y_set = (y ^ h ^ (h >> 1) ^ 1) & 1
    x_set = (x ^ q ^ 1) & 1
    return (((h * 2 + q) * 2 + y_set) * 2 + x_set) * OWN + (group & (OWN - 1))


def sums_kernel(
    labels_hbm,
    lib_hbm,
    counts_hbm,
    out_ref,
    labels_ref,
    lib_ref,
    counts_ref,
    members_ref,
    rows_ref,
    small_sems,
    sems,
):
    blocks, cells, width = counts_ref.shape
    tiles = width // LANES
    span = tiles * TILES * OWN
    part = TILE * OWN
    chunk = 2 * part
    core = lax.axis_index("gene") & 1
    end = blocks * span

    def arriving(b):
        columns = pl.ds(pl.multiple_of(b * width, width), width)
        return pltpu.make_async_copy(counts_hbm.at[:, columns], counts_ref.at[b], sems.at[b])

    labels_copy = pltpu.make_async_copy(labels_hbm, labels_ref, small_sems.at[0])
    lib_copy = pltpu.make_async_copy(lib_hbm, lib_ref, small_sems.at[1])
    labels_copy.start()
    lib_copy.start()

    @pl.loop(0, blocks)
    def _(b):
        arriving(b).start()

    labels_copy.wait()
    rows_ref[...] = row_of(labels_ref[...].reshape(1, cells), core)

    @pl.loop(0, G // chunk)
    def _(i):
        at = pl.multiple_of(i * chunk, chunk)
        row = lax.broadcasted_iota(jnp.int32, (chunk, cells), 0) + at
        members_ref[pl.ds(at, chunk), :] = (row == rows_ref[...]).astype(F32).astype(BF16)

    lib_copy.wait()
    size = lib_ref[...].reshape(1, cells)
    low = size & 255
    lane = lax.broadcasted_iota(jnp.int32, (LANES, cells), 0)
    sizes = jnp.where(lane & 4 == 0, size - low, low).astype(F32).astype(BF16)
    total = lax.dot_general(members_ref[...], sizes, (((1,), (1,)), ((), ())), preferred_element_type=F32)
    placed = in_lanes(split3(total), lax.broadcasted_iota(jnp.int32, (G, LANES), 1) & 3)
    lane = lax.broadcasted_iota(jnp.int32, (part, LANES), 1) >> 3
    tile = jnp.zeros((part, LANES), F32)
    for h in range(TILES):
        tile = jnp.where(lane == h, placed[h * part : (h + 1) * part], tile)
    out_ref[:, end:, :] = tile.astype(BF16).reshape(TILE, OWN, LANES)

    @pl.loop(0, blocks)
    def _(b):
        arriving(b).wait()
        sums = jnp.dot(members_ref[...], counts_ref[b].astype(F32).astype(BF16), preferred_element_type=F32)
        sums = sums.astype(BF16)
        for t in range(tiles):
            for h in range(TILES):
                row = pl.multiple_of(b * span, span) + (t * TILES + h) * OWN
                block = sums[h * part : (h + 1) * part, t * LANES : (t + 1) * LANES]
                out_ref[:, pl.ds(row, OWN), :] = block.reshape(TILE, OWN, LANES)


def middle_kernel(got_ref, out_ref):
    tiles = (got_ref.shape[1] - OWN) // (TILES * OWN)

    def added(row):
        return sum(got_ref[m, row : row + OWN, :].astype(F32) for m in range(TILE))

    lane = lax.broadcasted_iota(jnp.int32, (OWN, LANES), 1)
    half_lane = lax.broadcasted_iota(jnp.int32, (HALF, LANES), 1)
    library = added(tiles * TILES * OWN)
    for h in range(TILES):
        for t in range(tiles):
            out_ref[h, t * OWN : (t + 1) * OWN, :] = added((t * TILES + h) * OWN).astype(BF16)
        mine = jnp.sum(jnp.where(lane >> 3 == h, library, 0.0), axis=1, keepdims=True)
        first = in_lanes(split3(mine[:HALF]), half_lane)
        second = in_lanes(split3(mine[HALF:]), half_lane - 4)
        out_ref[h, tiles * OWN :, :] = jnp.where(half_lane < 4, first, second).astype(BF16)


def project_kernel(got_ref, loadings_ref, out_ref, rows_ref):
    tiles = got_ref.shape[1] // OWN
    halves = loadings_ref.shape[1] // LANES

    def added(row, rows):
        return sum(got_ref[h, row : row + rows, :].astype(F32) for h in range(TILES))

    lane = lax.broadcasted_iota(jnp.int32, (HALF, LANES), 1)
    pieces = added(tiles * OWN, HALF)
    first = jnp.sum(jnp.where(lane < 4, pieces, 0.0), axis=1, keepdims=True)
    second = jnp.sum(jnp.where(lane < 4, 0.0, pieces), axis=1, keepdims=True)
    library = jnp.concatenate([first, second], axis=0)
    rows_ref[...] = jnp.zeros_like(rows_ref)
    profile = []
    for t in range(tiles):
        normalized = jnp.log(1.0 + 10000.0 * added(t * OWN, OWN) / library).astype(BF16)
        rows_ref[pl.ds(t, OWN, stride=OWN), :] = normalized.astype(F32)
        profile.append(normalized)
    scores = jnp.dot(jnp.concatenate(profile, axis=1), loadings_ref[...], preferred_element_type=F32)
    for p, piece in enumerate(split3(scores)):
        for k in range(halves):
            at = tiles + p * halves + k
            rows_ref[pl.ds(at, OWN, stride=OWN), :] = piece[:, k * LANES : (k + 1) * LANES]
    for j in range(OWN):
        out_ref[j] = rows_ref[j * OWN : (j + 1) * OWN, :].astype(BF16)


def finish_kernel(got_ref, profile_ref, scores_ref):
    halves = scores_ref.shape[1] // LANES
    tiles = profile_ref.shape[1] // (got_ref.shape[0] * LANES)
    total = jnp.zeros((OWN, LANES), F32)
    for source in range(got_ref.shape[0]):
        block = got_ref[source].astype(F32)
        total += block
        for t in range(tiles):
            at = (source * tiles + t) * LANES
            profile_ref[:, at : at + LANES] = block[t : t + 1].astype(BF16)
    for k in range(halves):
        scores_ref[:, k * LANES : (k + 1) * LANES] = sum(
            total[tiles + p * halves + k : tiles + p * halves + k + 1] for p in range(3)
        )


def local_sums(labels, library_size, counts):
    cells, genes = counts.shape
    tiles = genes // LANES
    width = 512
    return pl.pallas_call(
        sums_kernel,
        in_specs=[HBM, HBM, HBM],
        out_specs=VMEM,
        out_shape=pltpu.VMEM((TILE, tiles * TILES * OWN + OWN, LANES), BF16),
        scratch_shapes=[
            pltpu.VMEM((cells,), jnp.int32),
            pltpu.VMEM((cells,), jnp.int32),
            pltpu.VMEM((genes // width, cells, width), jnp.int32),
            pltpu.VMEM((G, cells), BF16),
            pltpu.VMEM((1, cells), jnp.int32),
            pltpu.SemaphoreType.DMA((2,)),
            pltpu.SemaphoreType.DMA((genes // width,)),
        ],
        compiler_params=pltpu.CompilerParams(vmem_limit_bytes=LIMIT),
    )(*(pltpu.with_memory_space_constraint(array, pltpu.HBM) for array in (labels, library_size, counts)))


def shards(labels, counts, library_size, loadings):
    cells, genes = counts.shape
    k = loadings.shape[1]
    tiles = genes // LANES
    sent = local_sums(labels, library_size, counts)
    got = lax.all_to_all(sent, ("dp", "gene"), 0, 0, tiled=True, axis_index_groups=FIRST)
    sent = pl.pallas_call(
        middle_kernel,
        in_specs=[VMEM],
        out_specs=VMEM,
        out_shape=jax.ShapeDtypeStruct((TILES, tiles * OWN + HALF, LANES), BF16),
        compiler_params=pltpu.CompilerParams(vmem_limit_bytes=LIMIT),
    )(got)
    got = lax.all_to_all(sent, ("dp", "gene"), 0, 0, tiled=True, axis_index_groups=SECOND)
    sent = pl.pallas_call(
        project_kernel,
        in_specs=[VMEM, VMEM],
        out_specs=VMEM,
        out_shape=jax.ShapeDtypeStruct((16, OWN, LANES), BF16),
        scratch_shapes=[pltpu.VMEM((16 * OWN, LANES), F32)],
        compiler_params=pltpu.CompilerParams(vmem_limit_bytes=LIMIT),
    )(got, loadings)
    got = lax.all_to_all(sent, "gene", 0, 0, tiled=True)
    return pl.pallas_call(
        finish_kernel,
        in_specs=[VMEM],
        out_specs=(VMEM, VMEM),
        out_shape=(
            jax.ShapeDtypeStruct((1, 16 * genes), BF16),
            jax.ShapeDtypeStruct((1, k), F32),
        ),
        compiler_params=pltpu.CompilerParams(vmem_limit_bytes=LIMIT),
    )(got)


def solution(mesh):
    placed = (P("dp"), P("dp", "gene"), P("dp"), P("gene", None))
    return jax.shard_map(
        shards,
        mesh=mesh,
        in_specs=placed,
        out_specs=(P(("dp", "gene"), None), P(("dp", "gene"), None)),
        check_vma=False,
    )
```

```python
import jax
import jax.numpy as jnp
from jax import lax
from jax.experimental import pallas as pl
from jax.experimental.pallas import tpu as pltpu
from jax.sharding import PartitionSpec as P

G = 512
F32 = jnp.float32
BF16 = jnp.bfloat16
LANES = 128
OWN = 16
Y_SETS = ((1, 2, 4, 7), (0, 3, 5, 6))
X_SETS = ((1, 2), (0, 3))
TILE, TILES = 4, 8


def origin(core):
    return 4 + 3 * core, 2 - core


def member(z, core, y, x):
    y_from, x_from = origin(core)
    return ((y + y_from) % 8 * 4 + (x + x_from) % 4) * 16 + z * 2 + core


FIRST = [
    [member(z, core, ys[h], xs[q]) for ys in Y_SETS for xs in X_SETS]
    for z in range(8)
    for core in range(2)
    for h in range(4)
    for q in range(2)
]
SECOND = [
    [member(z, core, ys[h], xs[q]) for h in range(4) for q in range(2)]
    for z in range(8)
    for core in range(2)
    for ys in Y_SETS
    for xs in X_SETS
]
VMEM = pl.BlockSpec(memory_space=pltpu.VMEM)
HBM = pl.BlockSpec(memory_space=pltpu.HBM)
LIMIT = 48 * 1024 * 1024


def split3(value):
    one = value.astype(BF16).astype(F32)
    two = (value - one).astype(BF16).astype(F32)
    return one, two, ((value - one) - two).astype(BF16).astype(F32)


def in_lanes(pieces, lane):
    return jnp.where(lane == 0, pieces[0], jnp.where(lane == 1, pieces[1], jnp.where(lane == 2, pieces[2], 0.0)))


def row_of(group, core):
    y_from, x_from = origin(core)
    y = ((group >> 6) - y_from) & 7
    x = ((group >> 4) - x_from) & 3
    h, q = y >> 1, x >> 1
    y_set = (y ^ h ^ (h >> 1) ^ 1) & 1
    x_set = (x ^ q ^ 1) & 1
    return (((h * 2 + q) * 2 + y_set) * 2 + x_set) * OWN + (group & (OWN - 1))


def sums_kernel(
    labels_hbm,
    lib_hbm,
    counts_hbm,
    out_ref,
    labels_ref,
    lib_ref,
    counts_ref,
    members_ref,
    rows_ref,
    small_sems,
    sems,
):
    blocks, cells, width = counts_ref.shape
    tiles = width // LANES
    span = tiles * TILES * OWN
    part = TILE * OWN
    chunk = 2 * part
    core = lax.axis_index("gene") & 1
    end = blocks * span

    def arriving(b):
        columns = pl.ds(pl.multiple_of(b * width, width), width)
        return pltpu.make_async_copy(counts_hbm.at[:, columns], counts_ref.at[b], sems.at[b])

    labels_copy = pltpu.make_async_copy(labels_hbm, labels_ref, small_sems.at[0])
    lib_copy = pltpu.make_async_copy(lib_hbm, lib_ref, small_sems.at[1])
    labels_copy.start()
    lib_copy.start()

    @pl.loop(0, blocks)
    def _(b):
        arriving(b).start()

    labels_copy.wait()
    rows_ref[...] = row_of(labels_ref[...].reshape(1, cells), core)

    @pl.loop(0, G // chunk)
    def _(i):
        at = pl.multiple_of(i * chunk, chunk)
        row = lax.broadcasted_iota(jnp.int32, (chunk, cells), 0) + at
        members_ref[pl.ds(at, chunk), :] = (row == rows_ref[...]).astype(F32).astype(BF16)

    lib_copy.wait()
    size = lib_ref[...].reshape(1, cells)
    low = size & 255
    lane = lax.broadcasted_iota(jnp.int32, (LANES, cells), 0)
    sizes = jnp.where(lane & 4 == 0, size - low, low).astype(F32).astype(BF16)
    total = lax.dot_general(members_ref[...], sizes, (((1,), (1,)), ((), ())), preferred_element_type=F32)
    placed = in_lanes(split3(total), lax.broadcasted_iota(jnp.int32, (G, LANES), 1) & 3)
    lane = lax.broadcasted_iota(jnp.int32, (part, LANES), 1) >> 3
    tile = jnp.zeros((part, LANES), F32)
    for h in range(TILES):
        tile = jnp.where(lane == h, placed[h * part : (h + 1) * part], tile)
    out_ref[:, end:, :] = tile.astype(BF16).reshape(TILE, OWN, LANES)

    @pl.loop(0, blocks)
    def _(b):
        arriving(b).wait()
        sums = jnp.dot(members_ref[...], counts_ref[b].astype(F32).astype(BF16), preferred_element_type=F32)
        sums = sums.astype(BF16)
        for t in range(tiles):
            for h in range(TILES):
                row = pl.multiple_of(b * span, span) + (t * TILES + h) * OWN
                block = sums[h * part : (h + 1) * part, t * LANES : (t + 1) * LANES]
                out_ref[:, pl.ds(row, OWN), :] = block.reshape(TILE, OWN, LANES)


def middle_kernel(got_ref, out_ref):
    tiles = (got_ref.shape[1] - OWN) // (TILES * OWN)

    def added(row):
        return sum(got_ref[m, row : row + OWN, :].astype(F32) for m in range(TILE))

    lane = lax.broadcasted_iota(jnp.int32, (OWN, LANES), 1)
    library = added(tiles * TILES * OWN)
    for h in range(TILES):
        for t in range(tiles):
            out_ref[h, t * OWN : (t + 1) * OWN, :] = added((t * TILES + h) * OWN).astype(BF16)
        mine = jnp.sum(jnp.where(lane >> 3 == h, library, 0.0), axis=1, keepdims=True)
        out_ref[h, tiles * OWN :, :] = in_lanes(split3(mine), lane).astype(BF16)


def project_kernel(got_ref, loadings_ref, out_ref, rows_ref):
    tiles = got_ref.shape[1] // OWN - 1
    halves = loadings_ref.shape[1] // LANES

    def added(t):
        return sum(got_ref[h, t * OWN : (t + 1) * OWN, :].astype(F32) for h in range(TILES))

    library = jnp.sum(added(tiles), axis=1, keepdims=True)
    rows_ref[...] = jnp.zeros_like(rows_ref)
    profile = []
    for t in range(tiles):
        normalized = jnp.log(1.0 + 10000.0 * added(t) / library).astype(BF16)
        rows_ref[pl.ds(t, OWN, stride=OWN), :] = normalized.astype(F32)
        profile.append(normalized)
    scores = jnp.dot(jnp.concatenate(profile, axis=1), loadings_ref[...], preferred_element_type=F32)
    for p, piece in enumerate(split3(scores)):
        for k in range(halves):
            at = tiles + p * halves + k
            rows_ref[pl.ds(at, OWN, stride=OWN), :] = piece[:, k * LANES : (k + 1) * LANES]
    for j in range(OWN):
        out_ref[j] = rows_ref[j * OWN : (j + 1) * OWN, :].astype(BF16)


def finish_kernel(got_ref, profile_ref, scores_ref):
    halves = scores_ref.shape[1] // LANES
    tiles = profile_ref.shape[1] // (got_ref.shape[0] * LANES)
    total = jnp.zeros((OWN, LANES), F32)
    for source in range(got_ref.shape[0]):
        block = got_ref[source].astype(F32)
        total += block
        for t in range(tiles):
            at = (source * tiles + t) * LANES
            profile_ref[:, at : at + LANES] = got_ref[source, t : t + 1, :]
    for k in range(halves):
        scores_ref[:, k * LANES : (k + 1) * LANES] = sum(
            total[tiles + p * halves + k : tiles + p * halves + k + 1] for p in range(3)
        )


def local_sums(labels, library_size, counts):
    cells, genes = counts.shape
    tiles = genes // LANES
    width = 512
    return pl.pallas_call(
        sums_kernel,
        in_specs=[HBM, HBM, HBM],
        out_specs=VMEM,
        out_shape=pltpu.VMEM((TILE, tiles * TILES * OWN + OWN, LANES), BF16),
        scratch_shapes=[
            pltpu.VMEM((cells,), jnp.int32),
            pltpu.VMEM((cells,), jnp.int32),
            pltpu.VMEM((genes // width, cells, width), jnp.int32),
            pltpu.VMEM((G, cells), BF16),
            pltpu.VMEM((1, cells), jnp.int32),
            pltpu.SemaphoreType.DMA((2,)),
            pltpu.SemaphoreType.DMA((genes // width,)),
        ],
        compiler_params=pltpu.CompilerParams(vmem_limit_bytes=LIMIT),
    )(*(pltpu.with_memory_space_constraint(array, pltpu.HBM) for array in (labels, library_size, counts)))


def shards(labels, counts, library_size, loadings):
    cells, genes = counts.shape
    k = loadings.shape[1]
    tiles = genes // LANES
    sent = local_sums(labels, library_size, counts)
    got = lax.all_to_all(sent, ("dp", "gene"), 0, 0, tiled=True, axis_index_groups=FIRST)
    sent = pl.pallas_call(
        middle_kernel,
        in_specs=[VMEM],
        out_specs=VMEM,
        out_shape=jax.ShapeDtypeStruct((TILES, tiles * OWN + OWN, LANES), BF16),
        compiler_params=pltpu.CompilerParams(vmem_limit_bytes=LIMIT),
    )(got)
    got = lax.all_to_all(sent, ("dp", "gene"), 0, 0, tiled=True, axis_index_groups=SECOND)
    sent = pl.pallas_call(
        project_kernel,
        in_specs=[VMEM, VMEM],
        out_specs=VMEM,
        out_shape=jax.ShapeDtypeStruct((16, OWN, LANES), BF16),
        scratch_shapes=[pltpu.VMEM((16 * OWN, LANES), F32)],
        compiler_params=pltpu.CompilerParams(vmem_limit_bytes=LIMIT),
    )(got, loadings)
    got = lax.all_to_all(sent, "gene", 0, 0, tiled=True)
    return pl.pallas_call(
        finish_kernel,
        in_specs=[VMEM],
        out_specs=(VMEM, VMEM),
        out_shape=(
            jax.ShapeDtypeStruct((1, 16 * genes), BF16),
            jax.ShapeDtypeStruct((1, k), F32),
        ),
        compiler_params=pltpu.CompilerParams(vmem_limit_bytes=LIMIT),
    )(got)


def solution(mesh):
    placed = (P("dp"), P("dp", "gene"), P("dp"), P("gene", None))
    return jax.shard_map(
        shards,
        mesh=mesh,
        in_specs=placed,
        out_specs=(P(("dp", "gene"), None), P(("dp", "gene"), None)),
        check_vma=False,
    )
```
